256 devices in a mesh: cell: 64 (over z_lo, x, y), narrow: 4 (over z_hi, core).
Axes of the slice: x: 4, y: 4, z: 8 (z_hi: 2, z_lo: 4; z = z_hi * 4 + z_lo), core: 2. Of those that a mesh axis runs over, the one named last changes fastest.
Arguments:
- snapshots: bfloat16 [32768, 4096], P('cell', 'narrow'), may hold values from -16 to 16
- cell_volume: float32 [32768], P('cell'), may hold values from 0.1 to 10
- mode_vectors: bfloat16 [4096, 512], P('narrow'), may hold values from -0.09375 to 0.09375
- mode_scale: float32 [512], replicated, may hold values from 0.25 to 4
- interp_weights: bfloat16 [4096, 4096], P('cell', 'narrow'), may hold values from -0.09375 to 0.09375
Outputs:
- gram_matrix: float32 [4096, 4096], P('cell', 'narrow')
- fields: bfloat16 [32768, 4096], P('cell', 'narrow')
The draws below stay inside these ranges and needn't reach their ends.
All inputs are finite; a program needn't handle non-finite values.
Results may differ from the reference program's by a relative error of at most 0.0064.
Values may be sent and summed in bfloat16 or wider, within the bound.
No kernel may reach another device: no remote copies, remote signals or barrier semaphores. Data moves between devices by JAX's collectives and lax.ppermute only.
A program may use at most 128 MiB of HBM per device.

```python
import math
import jax
import jax.numpy as jnp
from jax import lax

MODES = 512
CELLS = 32768
NSNAP = 4096
NCOND = 4096


def strengthened(drawn, key, source, target, shards_of, factor):
    def block_of(dim):
        return (jnp.arange(drawn.shape[dim]) // (drawn.shape[dim] // shards_of)).reshape((-1,) + (1,) * (drawn.ndim - 1 - dim))

    first = jax.random.permutation(key, shards_of)[block_of(target)]
    second = (block_of(target) + shards_of // 2) % shards_of
    return jnp.where((block_of(source) == first) | (block_of(source) == second), factor * drawn, drawn)


def block_levels(own_key, dims, split, low, top_value):
    factor_of = 1.0
    for position, blocks in split:
        steps = jax.random.uniform(jax.random.fold_in(jax.random.fold_in(own_key, 6), position), (blocks,), jnp.float32, low / len(split), top_value / len(split))
        factor_of = factor_of * jnp.repeat(jnp.exp(steps), dims[position] // blocks).reshape((-1,) + (1,) * (len(dims) - 1 - position))
    return factor_of


def gaussian(stream_key, shape, scale, most, split=(), dtype=jnp.bfloat16):
    factor_of = block_levels(stream_key, shape, split, -0.22, 0.18) if split else 1.0
    entries = jax.random.normal(stream_key, shape, jnp.float32) * scale * factor_of
    return jnp.minimum(jnp.maximum(entries, -most), most).astype(dtype)


def heavy_noise(rng, extent, spread, most, split, heavy, kind=jnp.bfloat16):
    entries = spread * jax.random.normal(rng, extent, jnp.float32)
    if split:
        entries = entries * block_levels(rng, extent, split, -0.22, 0.18)
    return jnp.clip(strengthened(entries, jax.random.fold_in(rng, 3), *heavy), -most, most).astype(kind)


def setup_inputs(seed: int = 0) -> dict:
    streams_of = jax.random.split(jax.random.key(seed), 6)
    return {
        "snapshots": heavy_noise(streams_of[0], (CELLS, NSNAP), 1.0, 16.0, ((0, 64), (1, 4)), (0, 1, 64, 4.0)),
        "cell_volume": jnp.clip(jnp.exp(math.log(10.0) - 4.6051702 * jax.random.uniform(streams_of[1], (CELLS,), jnp.float32) ** block_levels(streams_of[1], (CELLS,), ((0, 64),), -0.2, 0.2)), 0.1, 10.0),
        "mode_vectors": gaussian(streams_of[2], (NSNAP, MODES), NSNAP ** -0.5, 0.09375, ((0, 4),)),
        "mode_scale": jnp.clip(jnp.exp(jax.random.uniform(streams_of[3], (MODES,), jnp.float32, math.log(0.25), math.log(4.0))), 0.25, 4.0),
        "interp_weights": gaussian(streams_of[4], (NSNAP, NCOND), NSNAP ** -0.5, 0.09375, ((0, 64), (1, 4))),
    }


def reference(snapshots, cell_volume, mode_vectors, mode_scale, interp_weights):
    weighted = (snapshots.astype(jnp.float32) * cell_volume[:, None]).astype(jnp.bfloat16)
    gram_matrix = lax.dot_general(snapshots, weighted, (((0,), (0,)), ((), ())), preferred_element_type=jnp.float32) / CELLS
    summed = lax.dot_general(mode_vectors.astype(jnp.float32), gram_matrix, (((0,), (1,)), ((), ())), precision=lax.Precision.HIGHEST)
    coefficients = (mode_scale[:, None] * summed).astype(jnp.bfloat16)
    new_coeffs = jnp.dot(coefficients, interp_weights, preferred_element_type=jnp.float32).astype(jnp.bfloat16)
    mode_shapes = jnp.dot(snapshots, mode_vectors, preferred_element_type=jnp.float32).astype(jnp.bfloat16)
    fields = jnp.dot(mode_shapes, new_coeffs, preferred_element_type=jnp.float32).astype(jnp.bfloat16)
    return gram_matrix, fields
```

```python
import jax
import jax.numpy as jnp
from jax import lax
from jax.sharding import Mesh, PartitionSpec as P

F32, BF16 = jnp.float32, jnp.bfloat16
AXES = ("zl", "x", "y", "zh", "k")


def shift(a, axis, s):
    n = lax.axis_size(axis)
    return lax.ppermute(a, axis, [(i, (i + s) % n) for i in range(n)])


def pick(a, index, dim):
    return lax.dynamic_index_in_dim(a, index, dim, keepdims=False)


def scatter_sum(p, axis, dim, dtype=BF16):
    n, me = lax.axis_size(axis), lax.axis_index(axis)
    total = pick(p, me, dim).astype(F32)
    for s in (1, 3, 2):
        total += shift(pick(p, (me + s) % n, dim).astype(dtype), axis, s).astype(F32)
    return total


def gather(a, axis):
    n, me = lax.axis_size(axis), lax.axis_index(axis)
    out = jnp.zeros((n, *a.shape), a.dtype)
    for s in range(n):
        part = shift(a, axis, s) if s else a
        out = lax.dynamic_update_index_in_dim(out, part, (me - s) % n, 0)
    return out


def tdot(a, b):
    return lax.dot_general(a, b, (((0,), (0,)), ((), ())), preferred_element_type=F32)


def plane_scatter(a, b, dtype=F32):
    a = scatter_sum(a, "x", 0)
    b = scatter_sum(b, "y", 1)
    a = scatter_sum(a.astype(dtype), "y", 0, dtype)
    b = scatter_sum(b.astype(dtype), "x", 0, dtype)
    return a, b


def to_row_owner(a):
    total = 0.0
    for s in range(4):
        perm = []
        for d in range(256):
            zl, xy, n = d // 64, d // 4 % 16, d % 4
            perm.append((d, n * 64 + xy * 4 + (zl + s) % 4))
        total += lax.ppermute(a, AXES, perm).astype(F32)
    return total


def shards(snapshots, cell_volume, mode_vectors, mode_scale, interp_weights):
    zl, zh, k = (lax.axis_index(a) for a in ("zl", "zh", "k"))
    n = zh * 2 + k
    cells, snaps = snapshots.shape
    modes, conds = mode_vectors.shape[1], interp_weights.shape[1]
    total_cells = cells * 64
    half_s, half_m = snaps // 2, modes // 2
    rows = snaps // 16

    with jax.named_scope("shapes"):
        part = jnp.dot(snapshots, mode_vectors, preferred_element_type=F32).reshape(2, cells // 2, modes)
        mine = pick(part, k, 0) + shift(pick(part, 1 - k, 0), "k", 1)
        z_first = shift(snapshots[:, :half_s], "zh", 1)
        other = shift(mine.astype(BF16), "zh", 1)
        z_second_in, other = lax.optimization_barrier((snapshots[:, half_s:], other))
        z_second = shift(z_second_in, "zh", 1)
        mine = (mine + other.astype(F32)).astype(BF16)
        theirs = shift(mine, "k", 1)
        shapes = jnp.where(k == 0, jnp.stack([mine, theirs]), jnp.stack([theirs, mine])).reshape(cells, modes)

    with jax.named_scope("weighted"):
        weighted = (snapshots.astype(F32) * cell_volume[:, None]).astype(BF16)

    with jax.named_scope("coeffs"):
        part = tdot(weighted, shapes).astype(BF16).reshape(4, 4, rows, modes)
        ca, cb = plane_scatter(part[..., :half_m], part[..., half_m:])
        coeffs = to_row_owner(jnp.concatenate([ca, cb], 1).astype(BF16))
        coeffs = (coeffs * (mode_scale / total_cells)[None, :]).astype(BF16)

    with jax.named_scope("new_coeffs"):
        part = tdot(coeffs, interp_weights).astype(BF16).reshape(2, 4, 4, modes // 32, conds)
        na, nb = plane_scatter(part[0], part[1])
        own = jnp.stack([na, nb])
        sent = own.astype(BF16)
        for s in (1, 3, 2):
            own += shift(sent, "zl", s).astype(F32)
        own = own.astype(BF16)
        na = gather(gather(own[0], "y"), "x").reshape(half_m, conds)
        nb = gather(gather(own[1], "x"), "y").transpose(1, 0, 2, 3).reshape(half_m, conds)
        new_coeffs = jnp.concatenate([na, nb])

    with jax.named_scope("gram"):
        s_core = shift(snapshots, "k", 1)
        s_z = jnp.concatenate([z_first, z_second], 1)
        s_zc = shift(s_z, "k", 1)
        half_c = snaps // 2
        blocks = []
        for pair in ((snapshots, s_core), (s_z, s_zc)):
            left = jnp.concatenate(pair, 1)
            ga = tdot(left, weighted[:, :half_c]).astype(BF16).reshape(2, 4, 4, rows, half_c)
            gb = tdot(left, weighted[:, half_c:]).astype(BF16).reshape(2, 4, 4, rows, half_c)
            ga = scatter_sum(ga, "x", 1).astype(BF16)
            gb = scatter_sum(gb, "y", 2).astype(BF16)
            ga = scatter_sum(ga, "y", 1)
            gb = scatter_sum(gb, "x", 1)
            blocks.append(jnp.concatenate([ga, gb], 2))
        blocks = jnp.concatenate(blocks)
        gram = pick(blocks, n ^ zl, 0)
        for s in (1, 3, 2):
            gram += shift(pick(blocks, n ^ ((zl + s) % 4), 0).astype(BF16), "zl", s).astype(F32)
        gram = gram / total_cells

    fields = jnp.dot(shapes, new_coeffs, preferred_element_type=F32).astype(BF16)
    return gram, fields


def solution(mesh):
    fine = Mesh(mesh.devices.reshape(4, 4, 4, 2, 2), AXES)
    cell, narrow = ("zl", "x", "y"), ("zh", "k")
    return jax.shard_map(
        shards,
        mesh=fine,
        in_specs=(P(cell, narrow), P(cell), P(narrow, None), P(), P(cell, narrow)),
        out_specs=(P(cell, narrow), P(cell, narrow)),
        check_vma=False,
    )
```

```python
import jax
import jax.numpy as jnp
from jax import lax
from jax.sharding import Mesh, PartitionSpec as P

F32, BF16 = jnp.float32, jnp.bfloat16
AXES = ("zl", "x", "y", "zh", "k")
PLANE = ("x", "y")


def swap(a, axis):
    return lax.ppermute(a, axis, [(0, 1), (1, 0)])


def pick(a, index, dim):
    return lax.dynamic_index_in_dim(a, index, dim, keepdims=False)


def exchange(a, axis):
    return lax.all_to_all(a, axis, 0, 0, tiled=True)


def scatter_sum(a, axis):
    return jnp.sum(exchange(a, axis).astype(F32), 0)


def everyone(a, axis):
    return exchange(jnp.broadcast_to(a, (lax.axis_size(axis), *a.shape)), axis)


def tdot(a, b):
    return lax.dot_general(a, b, (((0,), (0,)), ((), ())), preferred_element_type=F32)


def to_row_owner(a):
    total = 0.0
    for s in range(4):
        perm = []
        for d in range(256):
            zl, xy, n = d // 64, d // 4 % 16, d % 4
            perm.append((d, n * 64 + xy * 4 + (zl + s) % 4))
        total += lax.ppermute(a, AXES, perm).astype(F32)
    return total


def shards(snapshots, cell_volume, mode_vectors, mode_scale, interp_weights):
    zl, zh, k = (lax.axis_index(a) for a in ("zl", "zh", "k"))
    n = zh * 2 + k
    cells, snaps = snapshots.shape
    modes, conds = mode_vectors.shape[1], interp_weights.shape[1]
    total_cells = cells * 64
    rows = snaps // 16

    with jax.named_scope("weighted"):
        weighted = (snapshots.astype(F32) * cell_volume[:, None]).astype(BF16)

    with jax.named_scope("shapes"):
        part = jnp.dot(snapshots, mode_vectors, preferred_element_type=F32).reshape(2, cells // 2, modes)
        mine = scatter_sum(part, "k")
        mine = (mine + swap(mine.astype(BF16), "zh").astype(F32)).astype(BF16)
        theirs = swap(mine, "k")
        shapes = jnp.where(k == 0, jnp.stack([mine, theirs]), jnp.stack([theirs, mine])).reshape(cells, modes)

    with jax.named_scope("gram"):
        s_core = swap(snapshots, "k")
        s_z = swap(snapshots, "zh")
        s_zc = swap(s_z, "k")
        blocks = []
        for left in (snapshots, s_core, s_z, s_zc):
            part = tdot(left, weighted).astype(BF16)
            blocks.append(lax.psum_scatter(part, PLANE, scatter_dimension=0, tiled=True))

    with jax.named_scope("coeffs"):
        part = tdot(weighted, shapes).astype(BF16).reshape(16, rows, modes)
        coeffs = to_row_owner(scatter_sum(part, PLANE).astype(BF16))
        coeffs = (coeffs * (mode_scale / total_cells)[None, :]).astype(BF16)

    with jax.named_scope("new_coeffs"):
        part = tdot(coeffs, interp_weights).astype(BF16).reshape(16, modes // 16, conds)
        part = scatter_sum(part, PLANE).astype(BF16)
        part = jnp.sum(everyone(part, "zl").astype(F32), 0).astype(BF16)
        new_coeffs = everyone(part, PLANE).reshape(modes, conds)

    with jax.named_scope("gram_z"):
        blocks = jnp.stack(blocks)
        blocks = jnp.stack([pick(blocks, n ^ z, 0) for z in range(4)])
        gram = scatter_sum(blocks, "zl") / total_cells

    with jax.named_scope("fields"):
        fields = jnp.dot(shapes, new_coeffs, preferred_element_type=F32).astype(BF16)
    return gram, fields


def solution(mesh):
    fine = Mesh(mesh.devices.reshape(4, 4, 4, 2, 2), AXES)
    cell, narrow = ("zl", "x", "y"), ("zh", "k")
    return jax.shard_map(
        shards,
        mesh=fine,
        in_specs=(P(cell, narrow), P(cell), P(narrow, None), P(), P(cell, narrow)),
        out_specs=(P(cell, narrow), P(cell, narrow)),
        check_vma=False,
    )
```

```python
import jax
import jax.numpy as jnp
from jax import lax
from jax.sharding import Mesh, PartitionSpec as P

F32, BF16 = jnp.float32, jnp.bfloat16
AXES = ("zl", "x", "y", "zh", "k")
PLANE = ("x", "y")


def together(*arrays):
    return lax.optimization_barrier(arrays)


def swap(a, axis):
    return lax.ppermute(a, axis, [(0, 1), (1, 0)])


def pick(a, index, dim):
    return lax.dynamic_index_in_dim(a, index, dim, keepdims=False)


def exchange(a, axis):
    return lax.all_to_all(a, axis, 0, 0, tiled=True)


def scatter_sum(a, axis):
    return jnp.sum(exchange(a, axis).astype(F32), 0)


def ring_sum(a, axis, dim):
    n, me = lax.axis_size(axis), lax.axis_index(axis)
    total = pick(a, me, dim).astype(F32)
    for s in (1, 3, 2):
        perm = [(i, (i + s) % n) for i in range(n)]
        total += lax.ppermute(pick(a, (me + s) % n, dim), axis, perm).astype(F32)
    return total


def everyone(a, axis):
    return exchange(jnp.broadcast_to(a, (lax.axis_size(axis), *a.shape)), axis)


def tdot(a, b):
    return lax.dot_general(a, b, (((0,), (0,)), ((), ())), preferred_element_type=F32)


def to_row_owner(a):
    total = 0.0
    for s in range(4):
        perm = []
        for d in range(256):
            zl, xy, n = d // 64, d // 4 % 16, d % 4
            perm.append((d, n * 64 + xy * 4 + (zl + s) % 4))
        total += lax.ppermute(a, AXES, perm).astype(F32)
    return total


def shards(snapshots, cell_volume, mode_vectors, mode_scale, interp_weights):
    zl, zh, k = (lax.axis_index(a) for a in ("zl", "zh", "k"))
    n = zh * 2 + k
    cells, snaps = snapshots.shape
    modes, conds = mode_vectors.shape[1], interp_weights.shape[1]
    total_cells = cells * 64
    rows, half = snaps // 16, snaps // 2

    def gram_first(*lefts):
        left = jnp.concatenate(lefts, 1)
        a = tdot(left, weighted[:, :half]).astype(BF16).reshape(2, 4, 4, rows, half)
        b = tdot(left, weighted[:, half:]).astype(BF16).reshape(2, 4, 4, rows, half)
        return ring_sum(a, "x", 1).astype(BF16), ring_sum(b, "y", 2).astype(BF16)

    part = jnp.dot(snapshots, mode_vectors, preferred_element_type=F32).reshape(2, cells // 2, modes)
    s_z = swap(snapshots, "zh")
    mine = scatter_sum(part, "k")
    s_core = swap(snapshots, "k")
    weighted = (snapshots.astype(F32) * cell_volume[:, None]).astype(BF16)
    other = swap(mine.astype(BF16), "zh")
    mine, s_core, weighted = together(mine, s_core, weighted)
    a1, b1 = gram_first(snapshots, s_core)
    mine = (mine + other.astype(F32)).astype(BF16)
    theirs = swap(mine, "k")
    shapes = jnp.where(k == 0, jnp.stack([mine, theirs]), jnp.stack([theirs, mine])).reshape(cells, modes)

    part = tdot(weighted, shapes).astype(BF16).reshape(16, rows, modes)
    part = scatter_sum(part, PLANE).astype(BF16)
    part, a1, b1, s_z = together(part, a1, b1, s_z)

    s_zc = swap(s_z, "k")
    coeffs = to_row_owner(part)
    coeffs = (coeffs * (mode_scale / total_cells)[None, :]).astype(BF16)
    part = tdot(coeffs, interp_weights).astype(BF16).reshape(16, modes // 16, conds)
    part, s_zc = together(part, s_zc)

    a2, b2 = gram_first(s_z, s_zc)
    part = scatter_sum(part, PLANE).astype(BF16)
    part = jnp.sum(everyone(part, "zl").astype(F32), 0).astype(BF16)
    part, a2, b2 = together(part, a2, b2)

    new_coeffs = everyone(part, PLANE).reshape(modes, conds)
    a = ring_sum(jnp.concatenate([a1, a2]), "y", 1).astype(BF16)
    b = ring_sum(jnp.concatenate([b1, b2]), "x", 1).astype(BF16)
    blocks = jnp.concatenate([a, b], 2)
    new_coeffs, blocks = together(new_coeffs, blocks)

    blocks = jnp.stack([pick(blocks, n ^ z, 0) for z in range(4)])
    gram = scatter_sum(blocks, "zl") / total_cells
    fields = jnp.dot(shapes, new_coeffs, preferred_element_type=F32).astype(BF16)
    return gram, fields


def solution(mesh):
    fine = Mesh(mesh.devices.reshape(4, 4, 4, 2, 2), AXES)
    cell, narrow = ("zl", "x", "y"), ("zh", "k")
    return jax.shard_map(
        shards,
        mesh=fine,
        in_specs=(P(cell, narrow), P(cell), P(narrow, None), P(), P(cell, narrow)),
        out_specs=(P(cell, narrow), P(cell, narrow)),
        check_vma=False,
    )
```

```python
import jax
import jax.numpy as jnp
from jax import lax
from jax.sharding import Mesh, PartitionSpec as P

F32, BF16 = jnp.float32, jnp.bfloat16
AXES = ("zl", "x", "y", "zh", "k")
PLANE = ("x", "y")


def together(*arrays):
    return lax.optimization_barrier(arrays)


def swap(a, axis):
    return lax.ppermute(a, axis, [(0, 1), (1, 0)])


def pick(a, index, dim):
    return lax.dynamic_index_in_dim(a, index, dim, keepdims=False)


def exchange(a, axis):
    return lax.all_to_all(a, axis, 0, 0, tiled=True)


def scatter_sum(a, axis):
    return jnp.sum(exchange(a, axis).astype(F32), 0)


def ring_sum(a, axis, dim):
    n, me = lax.axis_size(axis), lax.axis_index(axis)
    total = pick(a, me, dim).astype(F32)
    for s in (1, 3, 2):
        perm = [(i, (i + s) % n) for i in range(n)]
        total += lax.ppermute(pick(a, (me + s) % n, dim), axis, perm).astype(F32)
    return total


def everyone(a, axis):
    return exchange(jnp.broadcast_to(a, (lax.axis_size(axis), *a.shape)), axis)


def tdot(a, b):
    return lax.dot_general(a, b, (((0,), (0,)), ((), ())), preferred_element_type=F32)


def to_row_owner(a):
    total = 0.0
    for s in range(4):
        perm = []
        for d in range(256):
            zl, xy, n = d // 64, d // 4 % 16, d % 4
            perm.append((d, n * 64 + xy * 4 + (zl + s) % 4))
        total += lax.ppermute(a, AXES, perm).astype(F32)
    return total


def shards(snapshots, cell_volume, mode_vectors, mode_scale, interp_weights):
    zl, zh, k = (lax.axis_index(a) for a in ("zl", "zh", "k"))
    n = zh * 2 + k
    cells, snaps = snapshots.shape
    modes, conds = mode_vectors.shape[1], interp_weights.shape[1]
    total_cells = cells * 64
    rows, half = snaps // 16, snaps // 2

    def gram_first(*lefts):
        left = jnp.concatenate(lefts, 1)
        a = tdot(left, weighted[:, :half]).astype(BF16).reshape(2, 4, 4, rows, half)
        b = tdot(left, weighted[:, half:]).astype(BF16).reshape(2, 4, 4, rows, half)
        return ring_sum(a, "x", 1).astype(BF16), ring_sum(b, "y", 2).astype(BF16)

    quarter = snaps // 4
    s_z0 = swap(snapshots[:, :quarter], "zh")
    part = jnp.dot(snapshots, mode_vectors, preferred_element_type=F32).reshape(2, cells // 2, modes)
    mine = scatter_sum(part, "k")
    s_core = swap(snapshots, "k")
    mine, s_z0 = together(mine, s_z0)
    other = swap(mine.astype(BF16), "zh")

    weighted = (snapshots.astype(F32) * cell_volume[:, None]).astype(BF16)
    weighted, s_core = together(weighted, s_core)
    part = tdot(jnp.concatenate([snapshots, s_core], 1), weighted).astype(BF16)
    part = part.reshape(2, 16, rows, snaps).transpose(1, 0, 2, 3).reshape(2 * snaps, snaps)
    mine, other, part, s_z1 = together(mine, other, part, snapshots[:, quarter:])
    g1 = lax.psum_scatter(part, PLANE, scatter_dimension=0, tiled=True).reshape(2, rows, snaps)

    s_z1 = swap(s_z1, "zh")
    mine = (mine + other.astype(F32)).astype(BF16)
    theirs = swap(mine, "k")
    shapes = jnp.where(k == 0, jnp.stack([mine, theirs]), jnp.stack([theirs, mine])).reshape(cells, modes)

    part = tdot(weighted, shapes).astype(BF16).reshape(16, rows, modes)
    part = scatter_sum(part, PLANE).astype(BF16)
    coeffs = to_row_owner(part)
    coeffs = (coeffs * (mode_scale / total_cells)[None, :]).astype(BF16)
    part = tdot(coeffs, interp_weights).astype(BF16).reshape(16, modes // 16, conds)
    part, s_z1 = together(part, s_z1)

    s_z = jnp.concatenate([s_z0, s_z1], 1)
    s_zc = swap(s_z, "k")
    a, b = gram_first(s_z, s_zc)
    part = scatter_sum(part, PLANE).astype(BF16)
    part = jnp.sum(everyone(part, "zl").astype(F32), 0).astype(BF16)
    part, a, b = together(part, a, b)

    new_coeffs = everyone(part, PLANE).reshape(modes, conds)
    a = ring_sum(a, "y", 1).astype(BF16)
    b = ring_sum(b, "x", 1).astype(BF16)
    g2 = jnp.concatenate([a, b], 2)
    new_coeffs, g2 = together(new_coeffs, g2)

    blocks = jnp.concatenate([g1, g2])
    blocks = jnp.stack([pick(blocks, n ^ z, 0) for z in range(4)])
    gram = scatter_sum(blocks, "zl") / total_cells
    fields = jnp.dot(shapes, new_coeffs, preferred_element_type=F32).astype(BF16)
    return gram, fields


def solution(mesh):
    fine = Mesh(mesh.devices.reshape(4, 4, 4, 2, 2), AXES)
    cell, narrow = ("zl", "x", "y"), ("zh", "k")
    return jax.shard_map(
        shards,
        mesh=fine,
        in_specs=(P(cell, narrow), P(cell), P(narrow, None), P(), P(cell, narrow)),
        out_specs=(P(cell, narrow), P(cell, narrow)),
        check_vma=False,
    )
```

```python
import jax
import jax.numpy as jnp
from jax import lax
from jax.sharding import Mesh, PartitionSpec as P

F32, BF16 = jnp.float32, jnp.bfloat16
AXES = ("zl", "x", "y", "zh", "k")
PLANE = ("x", "y")


def together(*arrays):
    return lax.optimization_barrier(arrays)


def swap(a, axis):
    return lax.ppermute(a, axis, [(0, 1), (1, 0)])


def pick(a, index, dim):
    return lax.dynamic_index_in_dim(a, index, dim, keepdims=False)


def exchange(a, axis):
    return lax.all_to_all(a, axis, 0, 0, tiled=True)


def scatter_sum(a, axis):
    return jnp.sum(exchange(a, axis).astype(F32), 0)


def ring_sum(a, axis, dim):
    n, me = lax.axis_size(axis), lax.axis_index(axis)
    total = pick(a, me, dim).astype(F32)
    for s in (1, 3, 2):
        perm = [(i, (i + s) % n) for i in range(n)]
        part = pick(a, (me + s) % n, dim).reshape(-1, a.shape[-1])
        total += lax.ppermute(part, axis, perm).reshape(total.shape).astype(F32)
    return total


def everyone(a, axis):
    return exchange(jnp.broadcast_to(a, (lax.axis_size(axis), *a.shape)), axis)


def tdot(a, b):
    return lax.dot_general(a, b, (((0,), (0,)), ((), ())), preferred_element_type=F32)


def to_row_owner(a):
    total = 0.0
    for s in range(4):
        perm = []
        for d in range(256):
            zl, xy, n = d // 64, d // 4 % 16, d % 4
            perm.append((d, n * 64 + xy * 4 + (zl + s) % 4))
        total += lax.ppermute(a, AXES, perm).astype(F32)
    return total


def shards(snapshots, cell_volume, mode_vectors, mode_scale, interp_weights):
    zl, zh, k = (lax.axis_index(a) for a in ("zl", "zh", "k"))
    n = zh * 2 + k
    cells, snaps = snapshots.shape
    modes, conds = mode_vectors.shape[1], interp_weights.shape[1]
    total_cells = cells * 64
    rows, half = snaps // 16, snaps // 2

    def gram_first(*lefts):
        left = jnp.concatenate(lefts, 1)
        a = tdot(left, weighted[:, :half]).astype(BF16).reshape(2, 4, 4, rows, half)
        b = tdot(left, weighted[:, half:]).astype(BF16).reshape(2, 4, 4, rows, half)
        return ring_sum(a, "x", 1).astype(BF16), ring_sum(b, "y", 2).astype(BF16)

    part = jnp.dot(snapshots, mode_vectors, preferred_element_type=F32).reshape(2, cells // 2, modes)
    mine = scatter_sum(part, "k")
    s_core = swap(snapshots, "k")
    other = swap(mine.astype(BF16), "zh")

    weighted = (snapshots.astype(F32) * cell_volume[:, None]).astype(BF16)
    weighted, s_core = together(weighted, s_core)
    part = tdot(jnp.concatenate([snapshots, s_core], 1), weighted).astype(BF16)
    part = part.reshape(2, 16, rows, snaps).transpose(1, 0, 2, 3).reshape(2 * snaps, snaps)
    mine, other, part, s_z = together(mine, other, part, snapshots)
    g1 = lax.psum_scatter(part, PLANE, scatter_dimension=0, tiled=True).reshape(2, rows, snaps)

    s_z = swap(s_z, "zh")
    mine = (mine + other.astype(F32)).astype(BF16)
    theirs = swap(mine, "k")
    shapes = jnp.where(k == 0, jnp.stack([mine, theirs]), jnp.stack([theirs, mine])).reshape(cells, modes)

    part = tdot(weighted, shapes).astype(BF16).reshape(16, rows, modes)
    part = scatter_sum(part, PLANE).astype(BF16)
    part, s_z = together(part, s_z)
    coeffs = to_row_owner(part)
    coeffs = (coeffs * (mode_scale / total_cells)[None, :]).astype(BF16)
    part = tdot(coeffs, interp_weights).astype(BF16).reshape(16, modes // 16, conds)

    s_zc = swap(s_z, "k")
    a, b = gram_first(s_z, s_zc)
    part = scatter_sum(part, PLANE).astype(BF16)
    part = jnp.sum(everyone(part, "zl").astype(F32), 0).astype(BF16)
    part, a, b = together(part, a, b)

    new_coeffs = everyone(part, PLANE).reshape(modes, conds)
    a = ring_sum(a, "y", 1).astype(BF16)
    b = ring_sum(b, "x", 1).astype(BF16)
    g2 = jnp.concatenate([a, b], 2)
    new_coeffs, g2 = together(new_coeffs, g2)

    blocks = jnp.concatenate([g1, g2])
    blocks = jnp.stack([pick(blocks, n ^ z, 0) for z in range(4)])
    gram = scatter_sum(blocks, "zl") / total_cells
    fields = jnp.dot(shapes, new_coeffs, preferred_element_type=F32).astype(BF16)
    return gram, fields


def solution(mesh):
    fine = Mesh(mesh.devices.reshape(4, 4, 4, 2, 2), AXES)
    cell, narrow = ("zl", "x", "y"), ("zh", "k")
    return jax.shard_map(
        shards,
        mesh=fine,
        in_specs=(P(cell, narrow), P(cell), P(narrow, None), P(), P(cell, narrow)),
        out_specs=(P(cell, narrow), P(cell, narrow)),
        check_vma=False,
    )
```

```python
import jax
import jax.numpy as jnp
from jax import lax
from jax.sharding import Mesh, PartitionSpec as P

F32, BF16 = jnp.float32, jnp.bfloat16
AXES = ("zl", "x", "y", "zh", "k")
PLANE = ("x", "y")


def together(*arrays):
    return lax.optimization_barrier(arrays)


def swap(a, axis):
    return lax.ppermute(a, axis, [(0, 1), (1, 0)])


def pick(a, index, dim):
    return lax.dynamic_index_in_dim(a, index, dim, keepdims=False)


def exchange(a, axis):
    return lax.all_to_all(a, axis, 0, 0, tiled=True)


def scatter_sum(a, axis):
    return jnp.sum(exchange(a, axis).astype(F32), 0)


def ring_sum(a, axis, dim):
    n, me = lax.axis_size(axis), lax.axis_index(axis)
    total = pick(a, me, dim).astype(F32)
    for s in (1, 3, 2):
        perm = [(i, (i + s) % n) for i in range(n)]
        part = pick(a, (me + s) % n, dim).reshape(-1, a.shape[-1])
        total += lax.ppermute(part, axis, perm).reshape(total.shape).astype(F32)
    return total


def everyone(a, axis):
    return exchange(jnp.broadcast_to(a, (lax.axis_size(axis), *a.shape)), axis)


def tdot(a, b):
    return lax.dot_general(a, b, (((0,), (0,)), ((), ())), preferred_element_type=F32)


def to_row_owner(a):
    total = 0.0
    for s in range(4):
        perm = []
        for d in range(256):
            zl, xy, n = d // 64, d // 4 % 16, d % 4
            perm.append((d, n * 64 + xy * 4 + (zl + s) % 4))
        total += lax.ppermute(a, AXES, perm).astype(F32)
    return total


def shards(snapshots, cell_volume, mode_vectors, mode_scale, interp_weights):
    zl, zh, k = (lax.axis_index(a) for a in ("zl", "zh", "k"))
    n = zh * 2 + k
    cells, snaps = snapshots.shape
    modes, conds = mode_vectors.shape[1], interp_weights.shape[1]
    total_cells = cells * 64
    rows, half = snaps // 16, snaps // 2

    def gram_y(*lefts):
        part = tdot(jnp.concatenate(lefts, 1), weighted).astype(BF16)
        return ring_sum(part.reshape(2, 2, 4, rows, snaps), "y", 2).astype(BF16)

    part = jnp.dot(snapshots, mode_vectors, preferred_element_type=F32).reshape(2, cells // 2, modes)
    mine = scatter_sum(part, "k")
    s_core = swap(snapshots, "k")
    other = swap(mine.astype(BF16), "zh")

    weighted = (snapshots.astype(F32) * cell_volume[:, None]).astype(BF16)
    weighted, s_core = together(weighted, s_core)
    part = tdot(jnp.concatenate([snapshots, s_core], 1), weighted).astype(BF16)
    part = part.reshape(2, 16, rows, snaps).transpose(1, 0, 2, 3).reshape(2 * snaps, snaps)
    mine, other, part, s_z0 = together(mine, other, part, snapshots[:, :half])
    g1 = lax.psum_scatter(part, PLANE, scatter_dimension=0, tiled=True).reshape(2, rows, snaps)

    s_z0 = swap(s_z0, "zh")
    mine = (mine + other.astype(F32)).astype(BF16)
    theirs = swap(mine, "k")
    shapes = jnp.where(k == 0, jnp.stack([mine, theirs]), jnp.stack([theirs, mine])).reshape(cells, modes)

    part = tdot(weighted, shapes).astype(BF16).reshape(16, rows, modes)
    part = scatter_sum(part, PLANE).astype(BF16)
    s_zc0 = swap(s_z0, "k")
    part, s_z0, s_zc0 = together(part, s_z0, s_zc0)
    coeffs = to_row_owner(part)
    coeffs = (coeffs * (mode_scale / total_cells)[None, :]).astype(BF16)
    coeffs, s_z1 = together(coeffs, snapshots[:, half:])
    s_z1 = swap(s_z1, "zh")
    g2a = gram_y(s_z0, s_zc0)
    part = tdot(coeffs, interp_weights).astype(BF16).reshape(16, modes // 16, conds)
    part = scatter_sum(part, PLANE).astype(BF16)
    s_zc1 = swap(s_z1, "k")
    part, s_z1, s_zc1, g2a = together(part, s_z1, s_zc1, g2a)

    g2b = gram_y(s_z1, s_zc1)
    part = jnp.sum(everyone(part, "zl").astype(F32), 0).astype(BF16)
    new_coeffs = everyone(part, PLANE).reshape(modes, conds)
    new_coeffs, g2b = together(new_coeffs, g2b)

    g2 = ring_sum(jnp.concatenate([g2a, g2b], 1), "x", 1).astype(BF16)
    blocks = jnp.concatenate([g1, g2])
    blocks = jnp.stack([pick(blocks, n ^ z, 0) for z in range(4)])
    gram = scatter_sum(blocks, "zl") / total_cells
    fields = jnp.dot(shapes, new_coeffs, preferred_element_type=F32).astype(BF16)
    return gram, fields


def solution(mesh):
    fine = Mesh(mesh.devices.reshape(4, 4, 4, 2, 2), AXES)
    cell, narrow = ("zl", "x", "y"), ("zh", "k")
    return jax.shard_map(
        shards,
        mesh=fine,
        in_specs=(P(cell, narrow), P(cell), P(narrow, None), P(), P(cell, narrow)),
        out_specs=(P(cell, narrow), P(cell, narrow)),
        check_vma=False,
    )
```

```python
import jax
import jax.numpy as jnp
from jax import lax
from jax.sharding import Mesh, PartitionSpec as P

F32, BF16 = jnp.float32, jnp.bfloat16
AXES = ("zl", "x", "y", "zh", "k")
PLANE = ("x", "y")


def together(*arrays):
    return lax.optimization_barrier(arrays)


def swap(a, axis):
    return lax.ppermute(a, axis, [(0, 1), (1, 0)])


def pick(a, index, dim):
    return lax.dynamic_index_in_dim(a, index, dim, keepdims=False)


def exchange(a, axis):
    return lax.all_to_all(a, axis, 0, 0, tiled=True)


def scatter_sum(a, axis):
    return jnp.sum(exchange(a, axis).astype(F32), 0)


def ring_sum(a, axis, dim):
    n, me = lax.axis_size(axis), lax.axis_index(axis)
    total = pick(a, me, dim).astype(F32)
    for s in (1, 3, 2):
        perm = [(i, (i + s) % n) for i in range(n)]
        part = pick(a, (me + s) % n, dim).reshape(-1, a.shape[-1])
        total += lax.ppermute(part, axis, perm).reshape(total.shape).astype(F32)
    return total


def everyone(a, axis):
    return exchange(jnp.broadcast_to(a, (lax.axis_size(axis), *a.shape)), axis)


def tdot(a, b):
    return lax.dot_general(a, b, (((0,), (0,)), ((), ())), preferred_element_type=F32)


def to_row_owner(a):
    total = 0.0
    for s in range(4):
        perm = []
        for d in range(256):
            zl, xy, n = d // 64, d // 4 % 16, d % 4
            perm.append((d, n * 64 + xy * 4 + (zl + s) % 4))
        total += lax.ppermute(a, AXES, perm).astype(F32)
    return total


def shards(snapshots, cell_volume, mode_vectors, mode_scale, interp_weights):
    zl, zh, k = (lax.axis_index(a) for a in ("zl", "zh", "k"))
    n = zh * 2 + k
    cells, snaps = snapshots.shape
    modes, conds = mode_vectors.shape[1], interp_weights.shape[1]
    total_cells = cells * 64
    rows, half = snaps // 16, snaps // 2

    part = jnp.dot(snapshots, mode_vectors, preferred_element_type=F32).reshape(2, cells // 2, modes)
    mine = scatter_sum(part, "k")
    s_core = swap(snapshots, "k")
    other = swap(mine.astype(BF16), "zh")

    weighted = (snapshots.astype(F32) * cell_volume[:, None]).astype(BF16)
    weighted, s_core = together(weighted, s_core)
    part = tdot(jnp.concatenate([snapshots, s_core], 1), weighted).astype(BF16)
    part = part.reshape(2, 16, rows, snaps).transpose(1, 0, 2, 3).reshape(2 * snaps, snaps)
    mine, other, part, s_z0 = together(mine, other, part, snapshots[:, :half])
    g1 = lax.psum_scatter(part, PLANE, scatter_dimension=0, tiled=True).reshape(2, rows, snaps)

    s_z0 = swap(s_z0, "zh")
    mine = (mine + other.astype(F32)).astype(BF16)
    theirs = swap(mine, "k")
    shapes = jnp.where(k == 0, jnp.stack([mine, theirs]), jnp.stack([theirs, mine])).reshape(cells, modes)

    part = tdot(weighted, shapes).astype(BF16).reshape(16, rows, modes)
    part = scatter_sum(part, PLANE).astype(BF16)
    s_zc0 = swap(s_z0, "k")
    part, s_z0, s_zc0 = together(part, s_z0, s_zc0)
    coeffs = to_row_owner(part)
    coeffs = (coeffs * (mode_scale / total_cells)[None, :]).astype(BF16)
    coeffs, s_z1 = together(coeffs, snapshots[:, half:])
    s_z1 = swap(s_z1, "zh")
    part = tdot(coeffs, interp_weights).astype(BF16).reshape(16, modes // 16, conds)
    part = scatter_sum(part, PLANE).astype(BF16)
    s_zc1 = swap(s_z1, "k")
    part, s_z1, s_zc1 = together(part, s_z1, s_zc1)

    left = jnp.concatenate([s_z0, s_z1, s_zc0, s_zc1], 1)
    a = tdot(left, weighted[:, :half]).astype(BF16)
    b = tdot(left, weighted[:, half:]).astype(BF16)
    part = jnp.sum(everyone(part, "zl").astype(F32), 0).astype(BF16)
    part, a, b = together(part, a, b)

    new_coeffs = everyone(part, PLANE).reshape(modes, conds)
    a = ring_sum(a.reshape(2, 4, 4, rows, half), "x", 1).astype(BF16)
    b = ring_sum(b.reshape(2, 4, 4, rows, half), "y", 2).astype(BF16)
    new_coeffs, a, b = together(new_coeffs, a, b)

    a = ring_sum(a, "y", 1).astype(BF16)
    b = ring_sum(b, "x", 1).astype(BF16)
    g2 = jnp.concatenate([a, b], 2)
    blocks = jnp.concatenate([g1, g2])
    blocks = jnp.stack([pick(blocks, n ^ z, 0) for z in range(4)])
    gram = scatter_sum(blocks, "zl") / total_cells
    fields = jnp.dot(shapes, new_coeffs, preferred_element_type=F32).astype(BF16)
    return gram, fields


def solution(mesh):
    fine = Mesh(mesh.devices.reshape(4, 4, 4, 2, 2), AXES)
    cell, narrow = ("zl", "x", "y"), ("zh", "k")
    return jax.shard_map(
        shards,
        mesh=fine,
        in_specs=(P(cell, narrow), P(cell), P(narrow, None), P(), P(cell, narrow)),
        out_specs=(P(cell, narrow), P(cell, narrow)),
        check_vma=False,
    )
```

```python
import jax
import jax.numpy as jnp
from jax import lax
from jax.sharding import Mesh, PartitionSpec as P

F32, BF16 = jnp.float32, jnp.bfloat16
AXES = ("zl", "x", "y", "zh", "k")
PLANE = ("x", "y")


def together(*arrays):
    return lax.optimization_barrier(arrays)


def swap(a, axis):
    return lax.ppermute(a, axis, [(0, 1), (1, 0)])


def pick(a, index, dim):
    return lax.dynamic_index_in_dim(a, index, dim, keepdims=False)


def exchange(a, axis):
    return lax.all_to_all(a, axis, 0, 0, tiled=True)


def scatter_sum(a, axis):
    return jnp.sum(exchange(a, axis).astype(F32), 0)


def ring_sum(a, axis, dim):
    n, me = lax.axis_size(axis), lax.axis_index(axis)
    total = pick(a, me, dim).astype(F32)
    for s in (1, 3, 2):
        perm = [(i, (i + s) % n) for i in range(n)]
        part = pick(a, (me + s) % n, dim).reshape(-1, a.shape[-1])
        total += lax.ppermute(part, axis, perm).reshape(total.shape).astype(F32)
    return total


def everyone(a, axis):
    return exchange(jnp.broadcast_to(a, (lax.axis_size(axis), *a.shape)), axis)


def tdot(a, b):
    return lax.dot_general(a, b, (((0,), (0,)), ((), ())), preferred_element_type=F32)


def to_row_owner(a):
    total = 0.0
    for s in range(4):
        perm = []
        for d in range(256):
            zl, xy, n = d // 64, d // 4 % 16, d % 4
            perm.append((d, n * 64 + xy * 4 + (zl + s) % 4))
        total += lax.ppermute(a, AXES, perm).astype(F32)
    return total


def shards(snapshots, cell_volume, mode_vectors, mode_scale, interp_weights):
    zl, zh, k = (lax.axis_index(a) for a in ("zl", "zh", "k"))
    n = zh * 2 + k
    cells, snaps = snapshots.shape
    modes, conds = mode_vectors.shape[1], interp_weights.shape[1]
    total_cells = cells * 64
    rows, half = snaps // 16, snaps // 2

    def products(*lefts):
        left = jnp.concatenate(lefts, 1)
        return tuple(tdot(left, w).astype(BF16) for w in (weighted[:, :half], weighted[:, half:]))

    def first_sums(a, b):
        a, b = (t.reshape(2, 4, 4, rows, half) for t in (a, b))
        return ring_sum(a, "x", 1).astype(BF16), ring_sum(b, "y", 2).astype(BF16)

    def second_sums(a, b):
        a, b = ring_sum(a, "y", 1).astype(BF16), ring_sum(b, "x", 1).astype(BF16)
        return jnp.concatenate([a, b], 2)

    part = jnp.dot(snapshots, mode_vectors, preferred_element_type=F32).reshape(2, cells // 2, modes)
    mine = scatter_sum(part, "k")
    s_core = swap(snapshots, "k")
    other = swap(mine.astype(BF16), "zh")

    weighted = (snapshots.astype(F32) * cell_volume[:, None]).astype(BF16)
    weighted, s_core = together(weighted, s_core)
    a, b = products(snapshots, s_core)
    mine, other, a, b, s_z0 = together(mine, other, a, b, snapshots[:, :half])
    a, b = first_sums(a, b)

    s_z0 = swap(s_z0, "zh")
    mine = (mine + other.astype(F32)).astype(BF16)
    theirs = swap(mine, "k")
    shapes = jnp.where(k == 0, jnp.stack([mine, theirs]), jnp.stack([theirs, mine])).reshape(cells, modes)

    part = tdot(weighted, shapes).astype(BF16).reshape(16, rows, modes)
    part = scatter_sum(part, PLANE).astype(BF16)
    s_zc0 = swap(s_z0, "k")
    part, s_z0, s_zc0, a, b = together(part, s_z0, s_zc0, a, b)
    coeffs = to_row_owner(part)
    coeffs = (coeffs * (mode_scale / total_cells)[None, :]).astype(BF16)
    g1 = second_sums(a, b)
    coeffs, s_z1, g1 = together(coeffs, snapshots[:, half:], g1)
    s_z1 = swap(s_z1, "zh")
    part = tdot(coeffs, interp_weights).astype(BF16).reshape(16, modes // 16, conds)
    part = scatter_sum(part, PLANE).astype(BF16)
    s_zc1 = swap(s_z1, "k")
    part, s_z1, s_zc1 = together(part, s_z1, s_zc1)

    a, b = products(s_z0, s_z1, s_zc0, s_zc1)
    part = jnp.sum(everyone(part, "zl").astype(F32), 0).astype(BF16)
    part, a, b = together(part, a, b)

    new_coeffs = everyone(part, PLANE).reshape(modes, conds)
    a, b = first_sums(a, b)
    new_coeffs, a, b = together(new_coeffs, a, b)
    g2 = second_sums(a, b)

    blocks = jnp.concatenate([g1, g2])
    blocks = jnp.stack([pick(blocks, n ^ z, 0) for z in range(4)])
    gram = scatter_sum(blocks, "zl") / total_cells
    fields = jnp.dot(shapes, new_coeffs, preferred_element_type=F32).astype(BF16)
    return gram, fields


def solution(mesh):
    fine = Mesh(mesh.devices.reshape(4, 4, 4, 2, 2), AXES)
    cell, narrow = ("zl", "x", "y"), ("zh", "k")
    return jax.shard_map(
        shards,
        mesh=fine,
        in_specs=(P(cell, narrow), P(cell), P(narrow, None), P(), P(cell, narrow)),
        out_specs=(P(cell, narrow), P(cell, narrow)),
        check_vma=False,
    )
```

```python
import jax
import jax.numpy as jnp
from jax import lax
from jax.sharding import Mesh, PartitionSpec as P

F32, BF16 = jnp.float32, jnp.bfloat16
AXES = ("zl", "x", "y", "zh", "k")
PLANE = ("x", "y")


def together(*arrays):
    return lax.optimization_barrier(arrays)


def swap(a, axis):
    return lax.ppermute(a, axis, [(0, 1), (1, 0)])


def pick(a, index, dim):
    return lax.dynamic_index_in_dim(a, index, dim, keepdims=False)


def exchange(a, axis):
    return lax.all_to_all(a, axis, 0, 0, tiled=True)


def scatter_sum(a, axis):
    return jnp.sum(exchange(a, axis).astype(F32), 0)


def ring_sum(a, axis, dim):
    n, me = lax.axis_size(axis), lax.axis_index(axis)
    total = pick(a, me, dim).astype(F32)
    for s in (1, 3, 2):
        perm = [(i, (i + s) % n) for i in range(n)]
        part = pick(a, (me + s) % n, dim).reshape(-1, a.shape[-1])
        total += lax.ppermute(part, axis, perm).reshape(total.shape).astype(F32)
    return total


def everyone(a, axis):
    return exchange(jnp.broadcast_to(a, (lax.axis_size(axis), *a.shape)), axis)


def tdot(a, b):
    return lax.dot_general(a, b, (((0,), (0,)), ((), ())), preferred_element_type=F32)


def to_row_owner(a):
    total = 0.0
    for s in range(4):
        perm = []
        for d in range(256):
            zl, xy, n = d // 64, d // 4 % 16, d % 4
            perm.append((d, n * 64 + xy * 4 + (zl + s) % 4))
        total += lax.ppermute(a, AXES, perm).astype(F32)
    return total


def shards(snapshots, cell_volume, mode_vectors, mode_scale, interp_weights):
    zl, zh, k = (lax.axis_index(a) for a in ("zl", "zh", "k"))
    n = zh * 2 + k
    cells, snaps = snapshots.shape
    modes, conds = mode_vectors.shape[1], interp_weights.shape[1]
    total_cells = cells * 64
    rows, half = snaps // 16, snaps // 2

    part = jnp.dot(snapshots, mode_vectors, preferred_element_type=F32).reshape(2, cells // 2, modes)
    mine = scatter_sum(part, "k")
    s_core = swap(snapshots, "k")
    other = swap(mine.astype(BF16), "zh")

    weighted = (snapshots.astype(F32) * cell_volume[:, None]).astype(BF16)
    weighted, s_core = together(weighted, s_core)
    part = tdot(jnp.concatenate([snapshots, s_core], 1), weighted).astype(BF16)
    part = part.reshape(2, 16, rows, snaps).transpose(1, 0, 2, 3).reshape(2 * snaps, snaps)
    mine, other, part, s_z0 = together(mine, other, part, snapshots[:, :half])
    g1 = lax.psum_scatter(part, PLANE, scatter_dimension=0, tiled=True).reshape(2, rows, snaps)

    s_z0 = swap(s_z0, "zh")
    mine = (mine + other.astype(F32)).astype(BF16)
    theirs = swap(mine, "k")
    shapes = jnp.where(k == 0, jnp.stack([mine, theirs]), jnp.stack([theirs, mine])).reshape(cells, modes)

    part = tdot(weighted, shapes).astype(BF16).reshape(16, rows, modes)
    part = scatter_sum(part, PLANE).astype(BF16)
    s_zc0 = swap(s_z0, "k")
    part, s_z0, s_zc0 = together(part, s_z0, s_zc0)
    coeffs = to_row_owner(part)
    coeffs = (coeffs * (mode_scale / total_cells)[None, :]).astype(BF16)
    coeffs, s_z1 = together(coeffs, snapshots[:, half:])
    s_z1 = swap(s_z1, "zh")
    part = tdot(coeffs, interp_weights).astype(BF16).reshape(16, modes // 16, conds)
    part = scatter_sum(part, PLANE).astype(BF16)
    s_zc1 = swap(s_z1, "k")
    left = jnp.concatenate([s_z0, s_z1, s_zc0, s_zc1], 1)
    a = tdot(left, weighted[:, :half]).astype(BF16)
    b = tdot(left, weighted[:, half:]).astype(BF16)
    part, a, b = together(part, a, b)
    a = ring_sum(a.reshape(2, 4, 4, rows, half), "x", 1).astype(BF16)
    b = ring_sum(b.reshape(2, 4, 4, rows, half), "y", 2).astype(BF16)

    part = jnp.sum(everyone(part, "zl").astype(F32), 0).astype(BF16)
    new_coeffs = everyone(part, PLANE).reshape(modes, conds)

    a = ring_sum(a, "y", 1).astype(BF16)
    b = ring_sum(b, "x", 1).astype(BF16)
    g2 = jnp.concatenate([a, b], 2)
    new_coeffs, g2 = together(new_coeffs, g2)

    blocks = jnp.concatenate([g1, g2])
    blocks = jnp.stack([pick(blocks, n ^ z, 0) for z in range(4)])
    gram = scatter_sum(blocks, "zl") / total_cells
    fields = jnp.dot(shapes, new_coeffs, preferred_element_type=F32).astype(BF16)
    return gram, fields


def solution(mesh):
    fine = Mesh(mesh.devices.reshape(4, 4, 4, 2, 2), AXES)
    cell, narrow = ("zl", "x", "y"), ("zh", "k")
    return jax.shard_map(
        shards,
        mesh=fine,
        in_specs=(P(cell, narrow), P(cell), P(narrow, None), P(), P(cell, narrow)),
        out_specs=(P(cell, narrow), P(cell, narrow)),
        check_vma=False,
    )
```

```python
import jax
import jax.numpy as jnp
from jax import lax
from jax.sharding import Mesh, PartitionSpec as P

F32, BF16 = jnp.float32, jnp.bfloat16
AXES = ("zl", "x", "y", "zh", "k")
PLANE = ("x", "y")


def together(*arrays):
    return lax.optimization_barrier(arrays)


def swap(a, axis):
    return lax.ppermute(a, axis, [(0, 1), (1, 0)])


def pick(a, index, dim):
    return lax.dynamic_index_in_dim(a, index, dim, keepdims=False)


def exchange(a, axis):
    return lax.all_to_all(a, axis, 0, 0, tiled=True)


def scatter_sum(a, axis):
    return jnp.sum(exchange(a, axis).astype(F32), 0)


def ring_sum(a, axis, dim):
    n, me = lax.axis_size(axis), lax.axis_index(axis)
    total = pick(a, me, dim).astype(F32)
    for s in (1, 3, 2):
        perm = [(i, (i + s) % n) for i in range(n)]
        part = pick(a, (me + s) % n, dim).reshape(-1, a.shape[-1])
        total += lax.ppermute(part, axis, perm).reshape(total.shape).astype(F32)
    return total


def everyone(a, axis):
    return exchange(jnp.broadcast_to(a, (lax.axis_size(axis), *a.shape)), axis)


def tdot(a, b):
    return lax.dot_general(a, b, (((0,), (0,)), ((), ())), preferred_element_type=F32)


def to_row_owner(a):
    total = 0.0
    for s in range(4):
        perm = []
        for d in range(256):
            zl, xy, n = d // 64, d // 4 % 16, d % 4
            perm.append((d, n * 64 + xy * 4 + (zl + s) % 4))
        total += lax.ppermute(a, AXES, perm).astype(F32)
    return total


def shards(snapshots, cell_volume, mode_vectors, mode_scale, interp_weights):
    zl, zh, k = (lax.axis_index(a) for a in ("zl", "zh", "k"))
    n = zh * 2 + k
    cells, snaps = snapshots.shape
    modes, conds = mode_vectors.shape[1], interp_weights.shape[1]
    total_cells = cells * 64
    rows, half = snaps // 16, snaps // 2

    part = jnp.dot(snapshots, mode_vectors, preferred_element_type=F32).reshape(2, cells // 2, modes)
    mine = scatter_sum(part, "k")
    s_core = swap(snapshots, "k")
    other = swap(mine.astype(BF16), "zh")

    weighted = (snapshots.astype(F32) * cell_volume[:, None]).astype(BF16)
    weighted, s_core = together(weighted, s_core)
    part = tdot(jnp.concatenate([snapshots, s_core], 1), weighted).astype(BF16)
    part = part.reshape(2, 16, rows, snaps).transpose(1, 0, 2, 3).reshape(2 * snaps, snaps)
    mine, other, part, s_z = together(mine, other, part, snapshots)
    g1 = lax.psum_scatter(part, PLANE, scatter_dimension=0, tiled=True).reshape(2, rows, snaps)

    s_z = swap(s_z, "zh")
    mine = (mine + other.astype(F32)).astype(BF16)
    theirs = swap(mine, "k")
    shapes = jnp.where(k == 0, jnp.stack([mine, theirs]), jnp.stack([theirs, mine])).reshape(cells, modes)

    part = tdot(weighted, shapes).astype(BF16).reshape(16, rows, modes)
    part = scatter_sum(part, PLANE).astype(BF16)
    part, s_z = together(part, s_z)
    coeffs = to_row_owner(part)
    coeffs = (coeffs * (mode_scale / total_cells)[None, :]).astype(BF16)

    left = jnp.concatenate([s_z, swap(s_z, "k")], 1)
    a = tdot(left, weighted[:, :half]).astype(BF16)
    b = tdot(left, weighted[:, half:]).astype(BF16)
    coeffs, a, b = together(coeffs, a, b)
    a = ring_sum(a.reshape(2, 4, 4, rows, half), "x", 1).astype(BF16)
    b = ring_sum(b.reshape(2, 4, 4, rows, half), "y", 2).astype(BF16)

    part = tdot(coeffs, interp_weights).astype(BF16).reshape(16, modes // 16, conds)
    part = scatter_sum(part, PLANE).astype(BF16)
    part, a = together(part, a)

    part = jnp.sum(everyone(part, "zl").astype(F32), 0).astype(BF16)
    new_coeffs = everyone(part, PLANE).reshape(modes, conds)

    a = ring_sum(a, "y", 1).astype(BF16)
    b = ring_sum(b, "x", 1).astype(BF16)
    g2 = jnp.concatenate([a, b], 2)
    new_coeffs, g2 = together(new_coeffs, g2)

    blocks = jnp.concatenate([g1, g2])
    blocks = jnp.stack([pick(blocks, n ^ z, 0) for z in range(4)])
    gram = scatter_sum(blocks, "zl") / total_cells
    fields = jnp.dot(shapes, new_coeffs, preferred_element_type=F32).astype(BF16)
    return gram, fields


def solution(mesh):
    fine = Mesh(mesh.devices.reshape(4, 4, 4, 2, 2), AXES)
    cell, narrow = ("zl", "x", "y"), ("zh", "k")
    return jax.shard_map(
        shards,
        mesh=fine,
        in_specs=(P(cell, narrow), P(cell), P(narrow, None), P(), P(cell, narrow)),
        out_specs=(P(cell, narrow), P(cell, narrow)),
        check_vma=False,
    )
```

```python
import jax
import jax.numpy as jnp
from jax import lax
from jax.sharding import Mesh, PartitionSpec as P

F32, BF16 = jnp.float32, jnp.bfloat16
AXES = ("zl", "x", "y", "zh", "k")
PLANE = ("x", "y")


def together(*arrays):
    return lax.optimization_barrier(arrays)


def swap(a, axis):
    return lax.ppermute(a, axis, [(0, 1), (1, 0)])


def pick(a, index, dim):
    return lax.dynamic_index_in_dim(a, index, dim, keepdims=False)


def exchange(a, axis):
    return lax.all_to_all(a, axis, 0, 0, tiled=True)


def scatter_sum(a, axis):
    return jnp.sum(exchange(a, axis).astype(F32), 0)


def ring_sum(a, axis, dim):
    n, me = lax.axis_size(axis), lax.axis_index(axis)
    total = pick(a, me, dim).astype(F32)
    for s in (1, 3, 2):
        perm = [(i, (i + s) % n) for i in range(n)]
        part = pick(a, (me + s) % n, dim).reshape(-1, a.shape[-1])
        total += lax.ppermute(part, axis, perm).reshape(total.shape).astype(F32)
    return total


def everyone(a, axis):
    return exchange(jnp.broadcast_to(a, (lax.axis_size(axis), *a.shape)), axis)


def tdot(a, b):
    return lax.dot_general(a, b, (((0,), (0,)), ((), ())), preferred_element_type=F32)


def to_row_owner(a):
    total = 0.0
    for s in range(4):
        perm = []
        for d in range(256):
            zl, xy, n = d // 64, d // 4 % 16, d % 4
            perm.append((d, n * 64 + xy * 4 + (zl + s) % 4))
        total += lax.ppermute(a, AXES, perm).astype(F32)
    return total


def shards(snapshots, cell_volume, mode_vectors, mode_scale, interp_weights):
    zl, zh, k = (lax.axis_index(a) for a in ("zl", "zh", "k"))
    n = zh * 2 + k
    cells, snaps = snapshots.shape
    modes, conds = mode_vectors.shape[1], interp_weights.shape[1]
    total_cells = cells * 64
    rows, half = snaps // 16, snaps // 2

    part = jnp.dot(snapshots, mode_vectors, preferred_element_type=F32).reshape(2, cells // 2, modes)
    mine = scatter_sum(part, "k")
    s_core = swap(snapshots, "k")
    other = swap(mine.astype(BF16), "zh")

    weighted = (snapshots.astype(F32) * cell_volume[:, None]).astype(BF16)
    weighted, s_core = together(weighted, s_core)
    part = tdot(jnp.concatenate([snapshots, s_core], 1), weighted).astype(BF16)
    part = part.reshape(2, 16, rows, snaps).transpose(1, 0, 2, 3).reshape(2 * snaps, snaps)
    mine, other, part, s_z0 = together(mine, other, part, snapshots[:, :half])
    g1 = lax.psum_scatter(part, PLANE, scatter_dimension=0, tiled=True).reshape(2, rows, snaps)

    s_z0 = swap(s_z0, "zh")
    mine = (mine + other.astype(F32)).astype(BF16)
    theirs = swap(mine, "k")
    shapes = jnp.where(k == 0, jnp.stack([mine, theirs]), jnp.stack([theirs, mine])).reshape(cells, modes)

    part = tdot(weighted, shapes).astype(BF16).reshape(16, rows, modes)
    part = scatter_sum(part, PLANE).astype(BF16)
    s_zc0 = swap(s_z0, "k")
    part, s_z0, s_zc0 = together(part, s_z0, s_zc0)
    coeffs = to_row_owner(part)
    coeffs = (coeffs * (mode_scale / total_cells)[None, :]).astype(BF16)
    coeffs, s_z1 = together(coeffs, snapshots[:, half:])
    s_z1 = swap(s_z1, "zh")
    part = tdot(coeffs, interp_weights).astype(BF16).reshape(16, modes // 16, conds)
    part = scatter_sum(part, PLANE).astype(BF16)
    s_zc1 = swap(s_z1, "k")
    left = jnp.concatenate([s_z0, s_z1, s_zc0, s_zc1], 1)
    a = tdot(left, weighted[:, :half]).astype(BF16)
    b = tdot(left, weighted[:, half:]).astype(BF16)
    part, a, b = together(part, a, b)
    a = ring_sum(a.reshape(2, 4, 4, rows, half), "x", 1).astype(BF16)
    b = ring_sum(b.reshape(2, 4, 4, rows, half), "y", 2).astype(BF16)

    part = jnp.sum(everyone(part, "zl").astype(F32), 0).astype(BF16)
    part = together(part, a)[0]
    new_coeffs = everyone(part, PLANE).reshape(modes, conds)

    a = ring_sum(a, "y", 1).astype(BF16)
    b = ring_sum(b, "x", 1).astype(BF16)
    g2 = jnp.concatenate([a, b], 2)
    blocks = jnp.concatenate([g1, g2])
    gram = pick(blocks, n ^ zl, 0).astype(F32)
    for s in (1, 3, 2):
        perm = [(i, (i + s) % 4) for i in range(4)]
        gram += lax.ppermute(pick(blocks, n ^ ((zl + s) % 4), 0), "zl", perm).astype(F32)
    gram = gram / total_cells
    fields = jnp.dot(shapes, new_coeffs, preferred_element_type=F32).astype(BF16)
    return gram, fields


def solution(mesh):
    fine = Mesh(mesh.devices.reshape(4, 4, 4, 2, 2), AXES)
    cell, narrow = ("zl", "x", "y"), ("zh", "k")
    return jax.shard_map(
        shards,
        mesh=fine,
        in_specs=(P(cell, narrow), P(cell), P(narrow, None), P(), P(cell, narrow)),
        out_specs=(P(cell, narrow), P(cell, narrow)),
        check_vma=False,
    )
```

```python
import jax
import jax.numpy as jnp
from jax import lax
from jax.sharding import Mesh, PartitionSpec as P

F32, BF16 = jnp.float32, jnp.bfloat16
AXES = ("zl", "x", "y", "zh", "k")
PLANE = ("x", "y")


def together(*arrays):
    return lax.optimization_barrier(arrays)


def swap(a, axis):
    return lax.ppermute(a, axis, [(0, 1), (1, 0)])


def pick(a, index, dim):
    return lax.dynamic_index_in_dim(a, index, dim, keepdims=False)


def exchange(a, axis):
    return lax.all_to_all(a, axis, 0, 0, tiled=True)


def scatter_sum(a, axis):
    return jnp.sum(exchange(a, axis).astype(F32), 0)


def ring_sum(a, axis, dim):
    n, me = lax.axis_size(axis), lax.axis_index(axis)
    total = pick(a, me, dim).astype(F32)
    for s in (1, 3, 2):
        perm = [(i, (i + s) % n) for i in range(n)]
        part = pick(a, (me + s) % n, dim).reshape(-1, a.shape[-1])
        total += lax.ppermute(part, axis, perm).reshape(total.shape).astype(F32)
    return total


def everyone(a, axis):
    return exchange(jnp.broadcast_to(a, (lax.axis_size(axis), *a.shape)), axis)


def tdot(a, b):
    return lax.dot_general(a, b, (((0,), (0,)), ((), ())), preferred_element_type=F32)


def to_row_owner(a):
    total = 0.0
    for s in range(4):
        perm = []
        for d in range(256):
            zl, xy, n = d // 64, d // 4 % 16, d % 4
            perm.append((d, n * 64 + xy * 4 + (zl + s) % 4))
        total += lax.ppermute(a, AXES, perm).astype(F32)
    return total


def shards(snapshots, cell_volume, mode_vectors, mode_scale, interp_weights):
    zl, zh, k = (lax.axis_index(a) for a in ("zl", "zh", "k"))
    n = zh * 2 + k
    cells, snaps = snapshots.shape
    modes, conds = mode_vectors.shape[1], interp_weights.shape[1]
    total_cells = cells * 64
    rows, half = snaps // 16, snaps // 2

    part = jnp.dot(snapshots, mode_vectors, preferred_element_type=F32).reshape(2, cells // 2, modes)
    mine = scatter_sum(part, "k")
    s_core = swap(snapshots, "k")
    other = swap(mine.astype(BF16), "zh")

    weighted = (snapshots.astype(F32) * cell_volume[:, None]).astype(BF16)
    weighted, s_core = together(weighted, s_core)
    part = tdot(jnp.concatenate([snapshots, s_core], 1), weighted).astype(BF16)
    part = part.reshape(2, 16, rows, snaps).transpose(1, 0, 2, 3).reshape(2 * snaps, snaps)
    mine, other, g1, s_z0 = together(mine, other, part, snapshots[:, :half])

    s_z0 = swap(s_z0, "zh")
    mine = (mine + other.astype(F32)).astype(BF16)
    theirs = swap(mine, "k")
    shapes = jnp.where(k == 0, jnp.stack([mine, theirs]), jnp.stack([theirs, mine])).reshape(cells, modes)

    part = tdot(weighted, shapes).astype(BF16).reshape(16, rows, modes)
    part = scatter_sum(part, PLANE).astype(BF16)
    s_zc0 = swap(s_z0, "k")
    part, s_z0, s_zc0, g1 = together(part, s_z0, s_zc0, g1)
    g1 = lax.psum_scatter(g1, PLANE, scatter_dimension=0, tiled=True).reshape(2, rows, snaps)
    coeffs = to_row_owner(part)
    coeffs = (coeffs * (mode_scale / total_cells)[None, :]).astype(BF16)
    coeffs, s_z1 = together(coeffs, snapshots[:, half:])
    s_z1 = swap(s_z1, "zh")
    part = tdot(coeffs, interp_weights).astype(BF16).reshape(16, modes // 16, conds)
    part = scatter_sum(part, PLANE).astype(BF16)
    s_zc1 = swap(s_z1, "k")
    left = jnp.concatenate([s_z0, s_z1, s_zc0, s_zc1], 1)
    a = tdot(left, weighted[:, :half]).astype(BF16)
    b = tdot(left, weighted[:, half:]).astype(BF16)
    part, a, b = together(part, a, b)
    a = ring_sum(a.reshape(2, 4, 4, rows, half), "x", 1).astype(BF16)
    b = ring_sum(b.reshape(2, 4, 4, rows, half), "y", 2).astype(BF16)

    part = jnp.sum(everyone(part, "zl").astype(F32), 0).astype(BF16)
    new_coeffs = everyone(part, PLANE).reshape(modes, conds)

    a = ring_sum(a, "y", 1).astype(BF16)
    b = ring_sum(b, "x", 1).astype(BF16)
    g2 = jnp.concatenate([a, b], 2)
    new_coeffs, g2 = together(new_coeffs, g2)

    blocks = jnp.concatenate([g1, g2])
    blocks = jnp.stack([pick(blocks, n ^ z, 0) for z in range(4)])
    gram = scatter_sum(blocks, "zl") / total_cells
    fields = jnp.dot(shapes, new_coeffs, preferred_element_type=F32).astype(BF16)
    return gram, fields


def solution(mesh):
    fine = Mesh(mesh.devices.reshape(4, 4, 4, 2, 2), AXES)
    cell, narrow = ("zl", "x", "y"), ("zh", "k")
    return jax.shard_map(
        shards,
        mesh=fine,
        in_specs=(P(cell, narrow), P(cell), P(narrow, None), P(), P(cell, narrow)),
        out_specs=(P(cell, narrow), P(cell, narrow)),
        check_vma=False,
    )
```

```python
import jax
import jax.numpy as jnp
from jax import lax
from jax.sharding import Mesh, PartitionSpec as P

F32, BF16 = jnp.float32, jnp.bfloat16
AXES = ("zl", "x", "y", "zh", "k")
PLANE = ("x", "y")


def together(*arrays):
    return lax.optimization_barrier(arrays)


def swap(a, axis):
    return lax.ppermute(a, axis, [(0, 1), (1, 0)])


def pick(a, index, dim):
    return lax.dynamic_index_in_dim(a, index, dim, keepdims=False)


def exchange(a, axis):
    return lax.all_to_all(a, axis, 0, 0, tiled=True)


def scatter_sum(a, axis):
    return jnp.sum(exchange(a, axis).astype(F32), 0)


def ring_sum(a, axis, dim):
    n, me = lax.axis_size(axis), lax.axis_index(axis)
    total = pick(a, me, dim).astype(F32)
    for s in (1, 3, 2):
        perm = [(i, (i + s) % n) for i in range(n)]
        part = pick(a, (me + s) % n, dim).reshape(-1, a.shape[-1])
        total += lax.ppermute(part, axis, perm).reshape(total.shape).astype(F32)
    return total


def everyone(a, axis):
    return exchange(jnp.broadcast_to(a, (lax.axis_size(axis), *a.shape)), axis)


def tdot(a, b):
    return lax.dot_general(a, b, (((0,), (0,)), ((), ())), preferred_element_type=F32)


def to_row_owner(a):
    total = 0.0
    for s in range(4):
        perm = []
        for d in range(256):
            zl, xy, n = d // 64, d // 4 % 16, d % 4
            perm.append((d, n * 64 + xy * 4 + (zl + s) % 4))
        total += lax.ppermute(a, AXES, perm).astype(F32)
    return total


def shards(snapshots, cell_volume, mode_vectors, mode_scale, interp_weights):
    zl, zh, k = (lax.axis_index(a) for a in ("zl", "zh", "k"))
    n = zh * 2 + k
    cells, snaps = snapshots.shape
    modes, conds = mode_vectors.shape[1], interp_weights.shape[1]
    total_cells = cells * 64
    rows, half = snaps // 16, snaps // 2

    part = jnp.dot(snapshots, mode_vectors, preferred_element_type=F32).reshape(2, cells // 2, modes)
    mine = scatter_sum(part, "k")
    s_core = swap(snapshots, "k")
    other = swap(mine.astype(BF16), "zh")

    weighted = (snapshots.astype(F32) * cell_volume[:, None]).astype(BF16)
    weighted, s_core = together(weighted, s_core)
    part = tdot(jnp.concatenate([snapshots, s_core], 1), weighted).astype(BF16)
    part = part.reshape(2, 16, rows, snaps).transpose(1, 0, 2, 3).reshape(2 * snaps, snaps)
    mine, other, part, s_z0 = together(mine, other, part, snapshots[:, :half])
    g1 = lax.psum_scatter(part, PLANE, scatter_dimension=0, tiled=True).reshape(2, rows, snaps)

    s_z0 = swap(s_z0, "zh")
    mine = (mine + other.astype(F32)).astype(BF16)
    theirs = swap(mine, "k")
    shapes = jnp.where(k == 0, jnp.stack([mine, theirs]), jnp.stack([theirs, mine])).reshape(cells, modes)

    part = tdot(weighted, shapes).astype(BF16).reshape(16, rows, modes)
    part = scatter_sum(part, PLANE).astype(BF16)
    s_zc0 = swap(s_z0, "k")
    part, s_z0, s_zc0 = together(part, s_z0, s_zc0)
    coeffs = to_row_owner(part)
    coeffs = (coeffs * (mode_scale / total_cells)[None, :]).astype(BF16)
    coeffs, s_z1 = together(coeffs, snapshots[:, half:])
    s_z1 = swap(s_z1, "zh")
    part = tdot(coeffs, interp_weights).astype(BF16).reshape(16, modes // 16, conds)
    part = scatter_sum(part, PLANE).astype(BF16)
    s_zc1 = swap(s_z1, "k")
    left = jnp.concatenate([s_z0, s_z1, s_zc0, s_zc1], 1)
    a = tdot(left, weighted[:, :half]).astype(BF16)
    b = tdot(left, weighted[:, half:]).astype(BF16)
    part, b = together(part, b)
    a = ring_sum(a.reshape(2, 4, 4, rows, half), "x", 1).astype(BF16)
    b = ring_sum(b.reshape(2, 4, 4, rows, half), "y", 2).astype(BF16)

    part = jnp.sum(everyone(part, "zl").astype(F32), 0).astype(BF16)
    new_coeffs = everyone(part, PLANE).reshape(modes, conds)

    a = ring_sum(a, "y", 1).astype(BF16)
    b = ring_sum(b, "x", 1).astype(BF16)
    g2 = jnp.concatenate([a, b], 2)
    new_coeffs, g2 = together(new_coeffs, g2)

    blocks = jnp.concatenate([g1, g2])
    blocks = jnp.stack([pick(blocks, n ^ z, 0) for z in range(4)])
    gram = scatter_sum(blocks, "zl") / total_cells
    fields = jnp.dot(shapes, new_coeffs, preferred_element_type=F32).astype(BF16)
    return gram, fields


def solution(mesh):
    fine = Mesh(mesh.devices.reshape(4, 4, 4, 2, 2), AXES)
    cell, narrow = ("zl", "x", "y"), ("zh", "k")
    return jax.shard_map(
        shards,
        mesh=fine,
        in_specs=(P(cell, narrow), P(cell), P(narrow, None), P(), P(cell, narrow)),
        out_specs=(P(cell, narrow), P(cell, narrow)),
        check_vma=False,
    )
```
